32 devices in a mesh: ctx: 16 (over z, y, x), head: 2 (over core).
Axes of the slice: x: 2, y: 2, z: 4, core: 2. Of those that a mesh axis runs over, the one named last changes fastest.
Arguments:
- tokens: bfloat16 [4096, 2048], P('ctx', 'head'), may hold values from -6 to 6
- qkv_weight: bfloat16 [2048, 3, 2048], P('ctx', None, 'head'), may hold values from -0.125 to 0.125
- out_gain: float32 [2048], P('head'), may hold values from 0.1 to 1.9
Outputs:
- attended: bfloat16 [4096, 2048], P('ctx', 'head')
The draws below stay inside these ranges and needn't reach their ends.
All inputs are finite; a program needn't handle non-finite values.
Results may differ from the reference program's by a relative error of at most 0.001.
Values may be sent and summed in bfloat16 or wider, within the bound.
A program may use at most 64 MiB of HBM per device.

```python
import math
import jax
import jax.numpy as jnp
from jax import lax

D = 2048
HEADS = 16
HD = 128
TOK_DEV = 256
TOKENS = 4096


def shard_levels(rng, shape, cuts, low, high):
    loudness = 1.0
    for position, blocks in cuts:
        steps = jax.random.uniform(jax.random.fold_in(jax.random.fold_in(rng, 6), position), (blocks,), jnp.float32, low / len(cuts), high / len(cuts))
        loudness = loudness * jnp.repeat(jnp.exp(steps), shape[position] // blocks).reshape((-1,) + (1,) * (len(shape) - 1 - position))
    return loudness


def centred(own_key, shape, width, reach, pieces=(), kind=jnp.bfloat16):
    values = width * jax.random.normal(own_key, shape, jnp.float32)
    if pieces:
        values = values * shard_levels(own_key, shape, pieces, -0.22, 0.18)
    return jnp.clip(values, -reach, reach).astype(kind)


def setup_inputs(seed: int = 0) -> dict:
    seeds = jax.random.split(jax.random.key(seed), 4)
    tokens = centred(seeds[0], (TOKENS, D), 1.0, 6.0, ((0, 16), (1, 2)))
    qkv_weight = centred(seeds[1], (D, 3, HEADS * HD), D ** -0.5, 0.125, ((0, 16), (2, 2)))
    out_gain = jnp.clip(1.0 + 0.18 * jax.random.normal(seeds[2], (HEADS * HD,), jnp.float32), 0.1, 1.9)
    return dict(tokens=tokens, qkv_weight=qkv_weight, out_gain=out_gain)


epsilon = 1e-06
highest = lax.Precision.HIGHEST

def block_terms(queries, key_rows, val_rows, prior_s, prior_m):
    rows_here = queries.shape[0]
    row_ids = lax.broadcasted_iota(jnp.int32, (rows_here, rows_here), 0)
    col_ids = lax.broadcasted_iota(jnp.int32, (rows_here, rows_here), 1)
    causal = row_ids >= col_ids
    strict = row_ids < col_ids
    scores = jnp.einsum('thd,shd->hts', queries, key_rows, precision=highest)
    lower_part = jnp.where(causal, scores, 0.0)
    pair_term = jnp.einsum('hti,hji->htj', lower_part, lower_part, precision=highest)
    query_state = jnp.einsum('thd,hde->the', queries, prior_s, precision=highest)
    cross_term = jnp.einsum('the,she->hts', query_state, queries, precision=highest)
    mixing = jnp.where(causal, pair_term + cross_term, 0.0)
    raw_out = jnp.einsum('hts,she->the', mixing, val_rows, precision=highest)
    raw_out = raw_out + jnp.einsum('thd,hde->the', queries, prior_m, precision=highest)
    local_s = jnp.einsum('thd,the->hde', key_rows, key_rows, precision=highest)
    local_c = jnp.einsum('thd,the->hde', queries, val_rows, precision=highest)
    upper_part = jnp.where(strict, scores, 0.0)
    weighted = jnp.einsum('hji,jhe->ihe', upper_part, val_rows, precision=highest)
    local_g = jnp.einsum('ihd,ihe->hde', key_rows, weighted, precision=highest)
    return (raw_out, local_s, local_c, local_g)

def reference(tokens, qkv_weight, out_gain):
    block_len = math.gcd(TOK_DEV, 128)
    blocks = TOKENS // block_len
    flat_weight = qkv_weight.reshape(D, 3 * HEADS * HD)
    token_blocks = tokens.reshape(blocks, block_len, D)

    def step(carry, token_block):
        prior_s, prior_c, prior_g = carry
        projected = jnp.dot(token_block, flat_weight, preferred_element_type=jnp.float32)
        projected = projected.reshape(block_len, 3, HEADS, HD)
        queries = projected[:, 0]
        key_rows = projected[:, 1]
        val_rows = projected[:, 2]
        prior_m = jnp.einsum('hij,hjk->hik', prior_s, prior_c, precision=highest) - prior_g
        raw_out, local_s, local_c, local_g = block_terms(queries, key_rows, val_rows, prior_s, prior_m)
        next_g = prior_g + local_g + jnp.einsum('hij,hjk->hik', local_s, prior_c, precision=highest)
        return ((prior_s + local_s, prior_c + local_c, next_g), raw_out)
    zeros_state = jnp.zeros((HEADS, HD, HD), jnp.float32)
    carry, raw_all = lax.scan(step, (zeros_state, zeros_state, zeros_state), token_blocks)
    raw_all = raw_all.reshape(TOKENS, HEADS, HD)
    mean_sq = lax.optimization_barrier(jnp.mean(raw_all * raw_all, axis=-1, keepdims=True))
    normed = raw_all * lax.rsqrt(mean_sq + epsilon) * out_gain.reshape(HEADS, HD)
    return normed.reshape(TOKENS, HEADS * HD).astype(jnp.bfloat16)
```

```python
import functools
import math

import jax
import jax.numpy as jnp
from jax import lax
from jax.experimental import pallas as pl
from jax.experimental.pallas import tpu as pltpu
from jax.sharding import PartitionSpec as P

HD = 128
GROUP = 4
BLOCK = 256

epsilon = 1e-06
MESH = pl.DeviceIdType.MESH
NN = (((1,), (0,)), ((), ()))
NT = (((1,), (1,)), ((), ()))
TN = (((0,), (0,)), ((), ()))


def split(x):
    high = x.astype(jnp.bfloat16)
    low = (x - high.astype(jnp.float32)).astype(jnp.bfloat16)
    return high, low


def dot(a, b, dims):
    one = functools.partial(
        lax.dot_general, dimension_numbers=dims, preferred_element_type=jnp.float32
    )
    return one(a[0], b[0]) + (one(a[0], b[1]) + one(a[1], b[0]))


def kernel(
    n, peers, group, x_ref, w_ref, gain_ref, out_ref,
    xbuf, wbuf, proj, ubuf, raw, s_own, s_in, r_own, r_in, state, result, landed,
    own_sem, wrecv, wa_send, wup, wdown, xrecv, xsend, xcore, ssend, srecv, rsend, rrecv, osend, orecv,
):
    me, e = lax.axis_index("ctx"), lax.axis_index("head")
    t, h = me // group, me % group
    turns = n // group
    toks, feats = x_ref.shape
    rows = w_ref.shape[1]
    width = wbuf.shape[2]
    heads = width // HD
    total = toks * group

    def ring(j):
        return (h + j) % group

    def other(o):
        return (e + o) % peers

    def at(tt, hh):
        return tt * group + hh

    barrier = pltpu.get_barrier_semaphore()
    for j in range(1, group):
        pl.semaphore_signal(barrier, inc=1, device_id=(at(t, ring(j)), e), device_id_type=MESH)
    for o in range(1, peers):
        pl.semaphore_signal(barrier, inc=1, device_id=(me, other(o)), device_id_type=MESH)

    @pl.loop(1, turns)
    def _(k):
        pl.semaphore_signal(
            barrier, inc=1, device_id=(at((t + k) % turns, h), e), device_id_type=MESH
        )

    pl.semaphore_wait(barrier, group - 1 + peers - 1 + turns - 1)

    def remote(src, dst, send, recv, to):
        return pltpu.make_async_remote_copy(
            src_ref=src, dst_ref=dst, send_sem=send, recv_sem=recv, device_id=to, device_id_type=MESH
        )

    def columns(hh):
        return pl.ds(pl.multiple_of(hh * width, width), width)

    def slot(s):
        return wbuf.at[:, pl.ds(pl.multiple_of(s * rows, rows), rows), :]

    def tok(hh):
        return pl.ds(pl.multiple_of(hh * toks, toks), toks)

    def xslot(hh, ee):
        return xbuf.at[tok(hh), pl.ds(pl.multiple_of(ee * feats, feats), feats)]

    def up(s):
        return remote(slot(s), slot(s), wup.at[s], wrecv.at[s], (at((t + 1) % turns, h), e))

    def down(s):
        return remote(
            slot(s), slot(s), wdown.at[s], wrecv.at[s], (at((t + turns - 1) % turns, h), e)
        )

    def across(j):
        hp = ring(j)
        return remote(w_ref.at[:, :, columns(hp)], slot(me), wa_send.at[j], wrecv.at[me], (at(t, hp), e))

    def xacross(j):
        return remote(x_ref, xslot(h, e), xsend.at[j], xrecv.at[h, e], (at(t, ring(j)), e))

    def xsibling(j, o):
        hs = ring(j)
        src = x_ref if j == 0 else xslot(hs, e)
        return remote(src, xslot(hs, e), xcore.at[j, o], xrecv.at[hs, e], (me, other(o)))

    w_own = pltpu.make_async_copy(w_ref.at[:, :, columns(h)], slot(me), own_sem.at[0])
    x_own = pltpu.make_async_copy(x_ref, xslot(h, e), own_sem.at[1])
    w_own.start()
    for j in range(1, group):
        across(j).start()
    x_own.start()
    w_own.wait()

    def send_up(s):
        @pl.when(t + 1 < turns)
        def _():
            up(s).start()

    def send_down(s):
        @pl.when(t > 0)
        def _():
            down(s).start()

    send_up(me)
    send_down(me)
    for j in range(1, group):
        xacross(j).start()
    for o in range(1, peers):
        xsibling(0, o).start()
    for j in range(1, group):
        s = at(t, ring(j))
        up(s).wait_recv()
        send_up(s)
        send_down(s)

    def arrive(d):
        for j in range(group):
            @pl.when(t - d >= 0)
            def _():
                s = at(t - d, ring(j))
                up(s).wait_recv()
                send_up(s)

            @pl.when(t + d < turns)
            def _():
                s = at(t + d, ring(j))
                down(s).wait_recv()
                send_down(s)

    first = min(2, turns)
    for d in range(1, first):
        arrive(d)

    x_own.wait()
    for j in range(1, group):
        remote(x_ref, xslot(ring(j), e), xsend.at[j], xrecv.at[ring(j), e], (me, other(1))).wait_recv()
        for o in range(1, peers):
            xsibling(j, o).start()
    for j in range(group):
        for o in range(1, peers):
            remote(
                x_ref, xslot(ring(j), other(o)), xcore.at[j, o], xrecv.at[ring(j), other(o)], (me, other(o))
            ).wait_recv()

    depth = rows * group

    def multiply(ts, fresh):
        ks = pl.ds(pl.multiple_of(ts * depth, depth), depth)

        @pl.loop(0, group)
        def _(m):
            block = xbuf[tok(m), ks]
            for c in range(3):
                part = lax.dot_general(
                    block, wbuf[c, ks, :], NN, preferred_element_type=jnp.float32
                )
                if fresh:
                    proj[c, tok(m), :] = part
                else:
                    proj[c, tok(m), :] += part

    def multiply_at(d):
        @pl.when(t - d >= 0)
        def _():
            multiply(t - d, False)

        @pl.when(t + d < turns)
        def _():
            multiply(t + d, False)

    if depth % 128 == 0:
        multiply(t, True)
        for d in range(1, first):
            multiply_at(d)

        @pl.loop(first, turns)
        def _(d):
            arrive(d)
            multiply_at(d)
    else:
        @pl.loop(first, turns)
        def _(d):
            arrive(d)

        @pl.loop(0, group)
        def _(m):
            for c in range(3):
                proj[c, tok(m), :] = lax.dot_general(
                    xbuf[tok(m), :], wbuf[c], NN, preferred_element_type=jnp.float32
                )

    blk = math.gcd(total, BLOCK)
    blocks = total // blk
    causal = lax.broadcasted_iota(jnp.int32, (blk, blk), 0) >= lax.broadcasted_iota(
        jnp.int32, (blk, blk), 1
    )

    def part(c, b, i):
        return split(proj[c, pl.ds(pl.multiple_of(b * blk, blk), blk), i * HD : (i + 1) * HD])

    def span(b):
        return pl.ds(pl.multiple_of(b * blk, blk), blk)

    def hcols(i):
        return slice(i * HD, (i + 1) * HD)

    def push(own, into, send, recv):
        def copy(tp):
            return remote(own, into.at[t], send.at[tp], recv.at[t], (at(tp, h), e))
        return copy

    s_push = push(s_own, s_in, ssend, srecv)
    r_push = push(r_own, r_in, rsend, rrecv)

    s_own[...] = jnp.zeros_like(s_own)

    @pl.loop(0, blocks)
    def _(b):
        for i in range(heads):
            keys = part(1, b, i)
            s_own[i] += dot(keys, keys, TN)

    @pl.loop(t + 1, turns)
    def _(tp):
        s_push(tp).start()

    state[...] = jnp.zeros_like(state)

    @pl.loop(0, blocks)
    def _(b):
        for i in range(heads):
            q, k = part(0, b, i), part(1, b, i)
            scores = jnp.where(causal, dot(q, k, NT), 0.0)
            ubuf[span(b), hcols(i)] = dot(split(scores), k, NN) + dot(q, split(state[i]), NN)
            state[i] += dot(k, k, TN)

    def earlier(own, into, recv):
        state[...] = jnp.zeros_like(state)

        @pl.loop(0, t)
        def _(ts):
            remote(own, into.at[ts], ssend.at[0], recv.at[ts], (at((t + 1) % turns, h), e)).wait_recv()
            state[...] += into[ts]

    earlier(s_own, s_in, srecv)
    r_own[...] = jnp.zeros_like(r_own)

    @pl.loop(0, blocks)
    def _(b):
        for i in range(heads):
            u = ubuf[span(b), hcols(i)] + dot(part(0, b, i), split(state[i]), NN)
            ubuf[span(b), hcols(i)] = u
            r_own[i] += dot(split(u), part(2, b, i), TN)

    @pl.loop(t + 1, turns)
    def _(tp):
        r_push(tp).start()

    state[...] = jnp.zeros_like(state)

    @pl.loop(0, blocks)
    def _(b):
        for i in range(heads):
            q, v = part(0, b, i), part(2, b, i)
            u = split(ubuf[span(b), hcols(i)])
            scores = jnp.where(causal, dot(q, u, NT), 0.0)
            raw[span(b), hcols(i)] = dot(split(scores), v, NN) + dot(q, split(state[i]), NN)
            state[i] += dot(u, v, TN)

    earlier(r_own, r_in, rrecv)

    def give(j):
        hp = ring(j)
        return remote(
            result.at[tok(hp), :], landed.at[:, columns(h)], osend.at[j], orecv.at[h], (at(t, hp), e)
        )

    for j in list(range(1, group)) + [0]:
        rs = tok(ring(j))
        for i in range(heads):
            full = raw[rs, hcols(i)] + dot(split(proj[0, rs, hcols(i)]), split(state[i]), NN)
            mean_sq = jnp.mean(full * full, axis=-1, keepdims=True)
            gain = gain_ref[:, pl.ds(pl.multiple_of(h * width + i * HD, HD), HD)]
            result[rs, hcols(i)] = (full * lax.rsqrt(mean_sq + epsilon) * gain).astype(jnp.bfloat16)
        if j:
            give(j).start()
    o_own = pltpu.make_async_copy(result.at[tok(h), :], landed.at[:, columns(h)], own_sem.at[2])
    o_own.start()

    for j in range(1, group):
        across(j).wait_send()
        xacross(j).wait_send()
    for j in range(group):
        for o in range(1, peers):
            xsibling(j, o).wait_send()

    @pl.when(t + 1 < turns)
    def _():
        @pl.loop(0, at(t + 1, 0))
        def _(s):
            up(s).wait_send()

    @pl.when(t > 0)
    def _():
        @pl.loop(at(t, 0), n)
        def _(s):
            down(s).wait_send()

    @pl.loop(t + 1, turns)
    def _(tp):
        s_push(tp).wait_send()
        r_push(tp).wait_send()

    o_own.wait()
    for j in range(1, group):
        give(j).wait_send()
        hs = ring(j)
        remote(
            result.at[tok(h), :], landed.at[:, columns(hs)], osend.at[j], orecv.at[hs], (at(t, hs), e)
        ).wait_recv()
    out_ref[...] = landed[...]


def body(tokens, qkv_weight, out_gain):
    n, peers = lax.axis_size("ctx"), lax.axis_size("head")
    toks, feats = tokens.shape
    rows, _, cols = qkv_weight.shape
    group = math.gcd(math.gcd(n, cols // HD), GROUP)
    turns = n // group
    width = cols // group
    heads = width // HD
    total = toks * group
    moments = (heads, HD, HD)
    f32, bf16 = jnp.float32, jnp.bfloat16
    dma = pltpu.SemaphoreType.DMA
    vmem = pl.BlockSpec(memory_space=pltpu.VMEM)
    return pl.pallas_call(
        functools.partial(kernel, n, peers, group),
        out_shape=jax.ShapeDtypeStruct((toks, cols), bf16),
        in_specs=[vmem] * 3,
        out_specs=vmem,
        scratch_shapes=[
            pltpu.VMEM((total, feats * peers), bf16),
            pltpu.VMEM((3, rows * n, width), bf16),
            pltpu.VMEM((3, total, width), f32),
            pltpu.VMEM((total, width), f32),
            pltpu.VMEM((total, width), f32),
            pltpu.VMEM(moments, f32),
            pltpu.VMEM((turns,) + moments, f32),
            pltpu.VMEM(moments, f32),
            pltpu.VMEM((turns,) + moments, f32),
            pltpu.VMEM(moments, f32),
            pltpu.VMEM((total, width), bf16),
            pltpu.VMEM((toks, cols), bf16),
            dma((3,)),
            dma((n,)),
            dma((group,)),
            dma((n,)),
            dma((n,)),
            dma((group, peers)),
            dma((group,)),
            dma((group, peers)),
            dma((turns,)),
            dma((turns,)),
            dma((turns,)),
            dma((turns,)),
            dma((group,)),
            dma((group,)),
        ],
        compiler_params=pltpu.CompilerParams(
            collective_id=0, has_side_effects=True, vmem_limit_bytes=48 * 1024 * 1024
        ),
    )(tokens, qkv_weight.transpose(1, 0, 2), out_gain.reshape(1, cols))


def solution(mesh):
    in_specs = (P("ctx", "head"), P("ctx", None, "head"), P("head"))
    out_specs = P("ctx", "head")
    return jax.shard_map(body, mesh=mesh, in_specs=in_specs, out_specs=out_specs, check_vma=False)
```

```python
import functools
import math

import jax
import jax.numpy as jnp
from jax import lax
from jax.experimental import pallas as pl
from jax.experimental.pallas import tpu as pltpu
from jax.sharding import PartitionSpec as P

HD = 128
GROUP = 4
BLOCK = 256

epsilon = 1e-06
MESH = pl.DeviceIdType.MESH
NN = (((1,), (0,)), ((), ()))
NT = (((1,), (1,)), ((), ()))
TN = (((0,), (0,)), ((), ()))


def split(x):
    high = x.astype(jnp.bfloat16)
    low = (x - high.astype(jnp.float32)).astype(jnp.bfloat16)
    return high, low


def dot(a, b, dims):
    one = functools.partial(
        lax.dot_general, dimension_numbers=dims, preferred_element_type=jnp.float32
    )
    return one(a[0], b[0]) + (one(a[0], b[1]) + one(a[1], b[0]))


def kernel(
    n, peers, group, x_ref, w_ref, gain_ref, out_ref,
    xbuf, wbuf, proj, ubuf, raw, s_own, s_in, r_own, r_in, result, landed,
    own_sem, slice_recv, slice_send, plane_recv, wup, wdown, xrecv, xsend, xcore,
    ssend, srecv, rsend, rrecv, osend, orecv,
):
    me, e = lax.axis_index("ctx"), lax.axis_index("head")
    t, h = me // group, me % group
    turns = n // group
    toks, feats = x_ref.shape
    rows = w_ref.shape[1]
    heads = wbuf.shape[0]
    width = heads * HD
    total = toks * group
    depth = rows * group
    order = (1, 0, 2)

    def ring(j):
        return (h + j) % group

    def other(o):
        return (e + o) % peers

    def at(tt, hh):
        return tt * group + hh

    barrier = pltpu.get_barrier_semaphore()
    for j in range(1, group):
        pl.semaphore_signal(barrier, inc=1, device_id=(at(t, ring(j)), e), device_id_type=MESH)
    for o in range(1, peers):
        pl.semaphore_signal(barrier, inc=1, device_id=(me, other(o)), device_id_type=MESH)

    @pl.loop(1, turns)
    def _(k):
        pl.semaphore_signal(
            barrier, inc=1, device_id=(at((t + k) % turns, h), e), device_id_type=MESH
        )

    pl.semaphore_wait(barrier, group - 1 + peers - 1 + turns - 1)

    def remote(src, dst, send, recv, to):
        return pltpu.make_async_remote_copy(
            src_ref=src, dst_ref=dst, send_sem=send, recv_sem=recv, device_id=to, device_id_type=MESH
        )

    def mcols(c):
        return slice(c * HD, (c + 1) * HD)

    def hcols(hh, i):
        return pl.ds(pl.multiple_of(hh * width + i * HD, HD), HD)

    def tok(hh):
        return pl.ds(pl.multiple_of(hh * toks, toks), toks)

    def kspan(ts):
        return pl.ds(pl.multiple_of(ts * depth, depth), depth)

    def slot(i, c, s):
        return wbuf.at[i, pl.ds(pl.multiple_of(s * rows, rows), rows), mcols(c)]

    def plane(i, c, ts):
        return wbuf.at[i, kspan(ts), mcols(c)]

    def across(i, c, j, s):
        hp = ring(j)
        return remote(
            w_ref.at[c, :, hcols(hp, i)], slot(i, c, s), slice_send.at[i, c, j],
            slice_recv.at[i, c, s % group], (at(t, hp), e),
        )

    def w_own(i, c):
        return pltpu.make_async_copy(w_ref.at[c, :, hcols(h, i)], slot(i, c, me), own_sem.at[i, c])

    def up(i, c, ts):
        p = plane(i, c, ts)
        return remote(p, p, wup.at[i, c, ts], plane_recv.at[i, c, ts], (at((t + 1) % turns, h), e))

    def down(i, c, ts):
        p = plane(i, c, ts)
        to = (at((t + turns - 1) % turns, h), e)
        return remote(p, p, wdown.at[i, c, ts], plane_recv.at[i, c, ts], to)

    def send_up(i, c, ts):
        @pl.when(t + 1 < turns)
        def _():
            up(i, c, ts).start()

    def send_down(i, c, ts):
        @pl.when(t > 0)
        def _():
            down(i, c, ts).start()

    def start_plane(i):
        for c in order:
            w_own(i, c).wait()
            for j in range(1, group):
                across(i, c, j, at(t, ring(j))).wait_recv()
            send_up(i, c, t)
            send_down(i, c, t)

    def arrive(i, d):
        for c in order:
            @pl.when(t - d >= 0)
            def _():
                up(i, c, t - d).wait_recv()
                send_up(i, c, t - d)

            @pl.when(t + d < turns)
            def _():
                down(i, c, t + d).wait_recv()
                send_down(i, c, t + d)

    def xslot(hh, ee):
        return xbuf.at[tok(hh), pl.ds(pl.multiple_of(ee * feats, feats), feats)]

    def xacross(j, hs):
        return remote(x_ref, xslot(hs, e), xsend.at[j], xrecv.at[hs, e], (at(t, ring(j)), e))

    def xsibling(j, o, ee):
        hs = ring(j)
        src = x_ref if j == 0 else xslot(hs, e)
        return remote(src, xslot(hs, ee), xcore.at[j, o], xrecv.at[hs, ee], (me, other(o)))

    x_own = pltpu.make_async_copy(x_ref, xslot(h, e), own_sem.at[heads, 0])

    def start_tokens():
        for j in range(1, group):
            xacross(j, h).start()
        for o in range(1, peers):
            xsibling(0, o, e).start()
        x_own.start()

    def finish_tokens():
        x_own.wait()
        for j in range(1, group):
            xacross(j, ring(j)).wait_recv()
            for o in range(1, peers):
                xsibling(j, o, e).start()
        for j in range(group):
            for o in range(1, peers):
                xsibling(j, o, other(o)).wait_recv()

    def multiply(i, ts, fresh):
        @pl.loop(0, group)
        def _(m):
            part = lax.dot_general(
                xbuf[tok(m), kspan(ts)], wbuf[i, kspan(ts), :], NN, preferred_element_type=jnp.float32
            )
            if fresh:
                proj[i, tok(m), :] = part
            else:
                proj[i, tok(m), :] += part

    def multiply_at(i, d):
        if d == 0:
            multiply(i, t, True)
            return

        @pl.when(t - d >= 0)
        def _():
            multiply(i, t - d, False)

        @pl.when(t + d < turns)
        def _():
            multiply(i, t + d, False)

    blk = math.gcd(total, BLOCK)
    blocks = total // blk
    causal = lax.broadcasted_iota(jnp.int32, (blk, blk), 0) >= lax.broadcasted_iota(
        jnp.int32, (blk, blk), 1
    )

    def over_blocks(f, first):
        if blocks > 4:
            return lax.fori_loop(0, blocks, f, first)
        for b in range(blocks):
            first = f(b, first)
        return first

    def span(b):
        return pl.ds(pl.multiple_of(b * blk, blk), blk)

    def part(i, c, b):
        return split(proj[i, span(b), mcols(c)])

    def push(own, into, send, recv, i, tp, ts):
        return remote(own.at[i], into.at[ts, i], send.at[i, tp], recv.at[i, ts], (at(tp, h), e))

    s_refs = (s_own, s_in, ssend, srecv)
    r_refs = (r_own, r_in, rsend, rrecv)
    zero = jnp.zeros((HD, HD), jnp.float32)

    def push_later(refs, i):
        @pl.loop(t + 1, turns)
        def _(tp):
            push(*refs, i, tp, t).start()

    def earlier(refs, i):
        def add(ts, sum_):
            push(*refs, i, (t + 1) % turns, ts).wait_recv()
            return sum_ + refs[1][ts, i]
        return lax.fori_loop(0, t, add, zero)

    def key_moments(i):
        def step(b, sum_):
            k = part(i, 1, b)
            return sum_ + dot(k, k, TN)
        s_own[i] = over_blocks(step, zero)
        push_later(s_refs, i)

    def local_keys(i):
        def step(b, sum_):
            q, k = part(i, 0, b), part(i, 1, b)
            scores = jnp.where(causal, dot(q, k, NT), 0.0)
            ubuf[i, span(b), :] = dot(split(scores), k, NN) + dot(q, split(sum_), NN)
            return sum_ + dot(k, k, TN)
        over_blocks(step, zero)

    def all_keys(i):
        before = split(earlier(s_refs, i))

        def step(b, sum_):
            u = ubuf[i, span(b), :] + dot(part(i, 0, b), before, NN)
            ubuf[i, span(b), :] = u
            return sum_ + dot(split(u), part(i, 2, b), TN)
        r_own[i] = over_blocks(step, zero)
        push_later(r_refs, i)

    def local_raw(i):
        def step(b, sum_):
            q, v, u = part(i, 0, b), part(i, 2, b), split(ubuf[i, span(b), :])
            scores = jnp.where(causal, dot(q, u, NT), 0.0)
            raw[i, span(b), :] = dot(split(scores), v, NN) + dot(q, split(sum_), NN)
            return sum_ + dot(u, v, TN)
        over_blocks(step, zero)

    def give(i, j, hh):
        hp = ring(j)
        return remote(
            result.at[i, tok(hp), :], landed.at[:, hcols(hh, i)], osend.at[i, j], orecv.at[i, hh],
            (at(t, hp), e),
        )

    def o_own(i):
        return pltpu.make_async_copy(
            result.at[i, tok(h), :], landed.at[:, hcols(h, i)], own_sem.at[heads, 1 + i]
        )

    def finish(i):
        before = split(earlier(r_refs, i))
        gain = gain_ref[:, hcols(h, i)]
        for j in list(range(1, group)) + [0]:
            rs = tok(ring(j))
            full = raw[i, rs, :] + dot(split(proj[i, rs, mcols(0)]), before, NN)
            mean_sq = jnp.mean(full * full, axis=-1, keepdims=True)
            result[i, rs, :] = (full * lax.rsqrt(mean_sq + epsilon) * gain).astype(jnp.bfloat16)
            (give(i, j, h) if j else o_own(i)).start()

    for i in range(heads):
        for c in order:
            w_own(i, c).start()
            for j in range(1, group):
                across(i, c, j, me).start()
    stages = (key_moments, local_keys, all_keys, local_raw, finish)
    if turns <= 8 and depth % 128 == 0:
        start_plane(0)
        start_tokens()
        for d in range(1, turns - 1):
            arrive(0, d)
        if heads > 1:
            start_plane(1)
        finish_tokens()
        for d in range(turns):
            if d == turns - 1 and d > 0:
                arrive(0, d)
            multiply_at(0, d)
        for i in range(heads):
            fill = []
            if i + 1 < heads:
                for d in range(turns):
                    if d + 1 < turns:
                        fill.append(functools.partial(arrive, i + 1, d + 1))
                    fill.append(functools.partial(multiply_at, i + 1, d))
            late = len(fill) - 4
            for stage in stages:
                stage(i)
                if len(fill) > late and len(fill) > 4:
                    fill.pop(0)()
                if stage is local_raw and i + 2 < heads:
                    start_plane(i + 2)
            for f in fill:
                f()
    else:
        start_tokens()
        for i in range(heads):
            start_plane(i)

            @pl.loop(1, turns)
            def _(d):
                arrive(i, d)
        finish_tokens()
        for i in range(heads):
            @pl.loop(0, group)
            def _(m):
                proj[i, tok(m), :] = lax.dot_general(
                    xbuf[tok(m), :], wbuf[i], NN, preferred_element_type=jnp.float32
                )
        for i in range(heads):
            for stage in stages:
                stage(i)

    for j in range(1, group):
        xacross(j, h).wait_send()
    for j in range(group):
        for o in range(1, peers):
            xsibling(j, o, e).wait_send()
    for i in range(heads):
        for c in order:
            for j in range(1, group):
                across(i, c, j, me).wait_send()

            @pl.when(t + 1 < turns)
            def _():
                @pl.loop(0, t + 1)
                def _(ts):
                    up(i, c, ts).wait_send()

            @pl.when(t > 0)
            def _():
                @pl.loop(t, turns)
                def _(ts):
                    down(i, c, ts).wait_send()

        @pl.loop(t + 1, turns)
        def _(tp):
            push(*s_refs, i, tp, t).wait_send()
            push(*r_refs, i, tp, t).wait_send()

        o_own(i).wait()
        for j in range(1, group):
            give(i, j, h).wait_send()
            give(i, j, ring(j)).wait_recv()
    out_ref[...] = landed[...]


def body(tokens, qkv_weight, out_gain):
    n, peers = lax.axis_size("ctx"), lax.axis_size("head")
    toks, feats = tokens.shape
    rows, _, cols = qkv_weight.shape
    group = math.gcd(math.gcd(n, cols // HD), GROUP)
    turns = n // group
    width = cols // group
    heads = width // HD
    total = toks * group
    moments = (heads, HD, HD)
    f32, bf16 = jnp.float32, jnp.bfloat16
    dma = pltpu.SemaphoreType.DMA
    vmem = pl.BlockSpec(memory_space=pltpu.VMEM)
    return pl.pallas_call(
        functools.partial(kernel, n, peers, group),
        out_shape=jax.ShapeDtypeStruct((toks, cols), bf16),
        in_specs=[pl.BlockSpec(memory_space=pl.ANY)] * 2 + [vmem],
        out_specs=vmem,
        scratch_shapes=[
            pltpu.VMEM((total, feats * peers), bf16),
            pltpu.VMEM((heads, rows * n, 3 * HD), bf16),
            pltpu.VMEM((heads, total, 3 * HD), f32),
            pltpu.VMEM((heads, total, HD), f32),
            pltpu.VMEM((heads, total, HD), f32),
            pltpu.VMEM(moments, f32),
            pltpu.VMEM((turns,) + moments, f32),
            pltpu.VMEM(moments, f32),
            pltpu.VMEM((turns,) + moments, f32),
            pltpu.VMEM((heads, total, HD), bf16),
            pltpu.VMEM((toks, cols), bf16),
            dma((heads + 1, max(3, heads + 1))),
            dma((heads, 3, group)),
            dma((heads, 3, group)),
            dma((heads, 3, turns)),
            dma((heads, 3, turns)),
            dma((heads, 3, turns)),
            dma((group, peers)),
            dma((group,)),
            dma((group, peers)),
            dma((heads, turns)),
            dma((heads, turns)),
            dma((heads, turns)),
            dma((heads, turns)),
            dma((heads, group)),
            dma((heads, group)),
        ],
        compiler_params=pltpu.CompilerParams(
            collective_id=0, has_side_effects=True, vmem_limit_bytes=48 * 1024 * 1024
        ),
    )(tokens, qkv_weight.transpose(1, 0, 2), out_gain.reshape(1, cols))


def solution(mesh):
    in_specs = (P("ctx", "head"), P("ctx", None, "head"), P("head"))
    out_specs = P("ctx", "head")
    return jax.shard_map(body, mesh=mesh, in_specs=in_specs, out_specs=out_specs, check_vma=False)
```

```python
import functools
import math

import jax
import jax.numpy as jnp
from jax import lax
from jax.experimental import pallas as pl
from jax.experimental.pallas import tpu as pltpu
from jax.sharding import PartitionSpec as P

HD = 128
GROUP = 4
BLOCK = 256

epsilon = 1e-06
MESH = pl.DeviceIdType.MESH
NN = (((1,), (0,)), ((), ()))
NT = (((1,), (1,)), ((), ()))
TN = (((0,), (0,)), ((), ()))


def split(x):
    high = x.astype(jnp.bfloat16)
    low = (x - high.astype(jnp.float32)).astype(jnp.bfloat16)
    return high, low


def dot(a, b, dims):
    one = functools.partial(
        lax.dot_general, dimension_numbers=dims, preferred_element_type=jnp.float32
    )
    return one(a[0], b[0]) + (one(a[0], b[1]) + one(a[1], b[0]))


def kernel(
    n, peers, group, x_ref, w_ref, gain_ref, out_ref,
    xbuf, wbuf, proj, ubuf, raw, s_own, s_in, r_own, r_in, result, landed,
    own_sem, slice_recv, slice_send, plane_recv, wup, wdown, xrecv, xsend, xcore,
    ssend, srecv, rsend, rrecv, osend, orecv,
):
    me, e = lax.axis_index("ctx"), lax.axis_index("head")
    t, h = me // group, me % group
    turns = n // group
    toks, feats = x_ref.shape
    rows = w_ref.shape[1]
    heads = wbuf.shape[0]
    width = heads * HD
    total = toks * group
    depth = rows * group
    order = (1, 0, 2)

    def ring(j):
        return (h + j) % group

    def other(o):
        return (e + o) % peers

    def at(tt, hh):
        return tt * group + hh

    barrier = pltpu.get_barrier_semaphore()
    for j in range(1, group):
        pl.semaphore_signal(barrier, inc=1, device_id=(at(t, ring(j)), e), device_id_type=MESH)
    for o in range(1, peers):
        pl.semaphore_signal(barrier, inc=1, device_id=(me, other(o)), device_id_type=MESH)

    @pl.loop(1, turns)
    def _(k):
        pl.semaphore_signal(
            barrier, inc=1, device_id=(at((t + k) % turns, h), e), device_id_type=MESH
        )

    pl.semaphore_wait(barrier, group - 1 + peers - 1 + turns - 1)

    def remote(src, dst, send, recv, to):
        return pltpu.make_async_remote_copy(
            src_ref=src, dst_ref=dst, send_sem=send, recv_sem=recv, device_id=to, device_id_type=MESH
        )

    def mcols(c):
        return slice(c * HD, (c + 1) * HD)

    def hcols(hh, i):
        return pl.ds(pl.multiple_of(hh * width + i * HD, HD), HD)

    def tok(hh):
        return pl.ds(pl.multiple_of(hh * toks, toks), toks)

    def kspan(ts):
        return pl.ds(pl.multiple_of(ts * depth, depth), depth)

    def slot(i, c, s):
        return wbuf.at[i, pl.ds(pl.multiple_of(s * rows, rows), rows), mcols(c)]

    def plane(i, c, ts):
        return wbuf.at[i, kspan(ts), mcols(c)]

    def across(i, c, j, s):
        hp = ring(j)
        return remote(
            w_ref.at[c, :, hcols(hp, i)], slot(i, c, s), slice_send.at[i, c, j],
            slice_recv.at[i, c, s % group], (at(t, hp), e),
        )

    def w_own(i, c):
        return pltpu.make_async_copy(w_ref.at[c, :, hcols(h, i)], slot(i, c, me), own_sem.at[i, c])

    def up(i, c, ts):
        p = plane(i, c, ts)
        return remote(p, p, wup.at[i, c, ts], plane_recv.at[i, c, ts], (at((t + 1) % turns, h), e))

    def down(i, c, ts):
        p = plane(i, c, ts)
        to = (at((t + turns - 1) % turns, h), e)
        return remote(p, p, wdown.at[i, c, ts], plane_recv.at[i, c, ts], to)

    def send_up(i, c, ts):
        @pl.when(t + 1 < turns)
        def _():
            up(i, c, ts).start()

    def send_down(i, c, ts):
        @pl.when(t > 0)
        def _():
            down(i, c, ts).start()

    def start_plane(i):
        for c in order:
            w_own(i, c).wait()
            for j in range(1, group):
                across(i, c, j, at(t, ring(j))).wait_recv()
            send_up(i, c, t)
            send_down(i, c, t)

    def arrive(i, d):
        for c in order:
            @pl.when(t - d >= 0)
            def _():
                up(i, c, t - d).wait_recv()
                send_up(i, c, t - d)

            @pl.when(t + d < turns)
            def _():
                down(i, c, t + d).wait_recv()
                send_down(i, c, t + d)

    def xslot(hh, ee):
        return xbuf.at[tok(hh), pl.ds(pl.multiple_of(ee * feats, feats), feats)]

    def xacross(j, hs):
        return remote(x_ref, xslot(hs, e), xsend.at[j], xrecv.at[hs, e], (at(t, ring(j)), e))

    def xsibling(j, o, ee):
        hs = ring(j)
        src = x_ref if j == 0 else xslot(hs, e)
        return remote(src, xslot(hs, ee), xcore.at[j, o], xrecv.at[hs, ee], (me, other(o)))

    x_own = pltpu.make_async_copy(x_ref, xslot(h, e), own_sem.at[heads, 0])

    def start_tokens():
        for j in range(1, group):
            xacross(j, h).start()
        for o in range(1, peers):
            xsibling(0, o, e).start()
        x_own.start()

    def finish_tokens():
        x_own.wait()
        for j in range(1, group):
            xacross(j, ring(j)).wait_recv()
            for o in range(1, peers):
                xsibling(j, o, e).start()
        for j in range(group):
            for o in range(1, peers):
                xsibling(j, o, other(o)).wait_recv()

    def multiply(i, ts, fresh):
        @pl.loop(0, group)
        def _(m):
            part = lax.dot_general(
                xbuf[tok(m), kspan(ts)], wbuf[i, kspan(ts), :], NN, preferred_element_type=jnp.float32
            )
            if fresh:
                proj[i, tok(m), :] = part
            else:
                proj[i, tok(m), :] += part

    def multiply_at(i, d):
        if d == 0:
            multiply(i, t, True)
            return

        @pl.when(t - d >= 0)
        def _():
            multiply(i, t - d, False)

        @pl.when(t + d < turns)
        def _():
            multiply(i, t + d, False)

    blk = math.gcd(total, BLOCK)
    blocks = total // blk
    causal = lax.broadcasted_iota(jnp.int32, (blk, blk), 0) >= lax.broadcasted_iota(
        jnp.int32, (blk, blk), 1
    )

    def over_blocks(f, first):
        if blocks > 4:
            return lax.fori_loop(0, blocks, f, first)
        for b in range(blocks):
            first = f(b, first)
        return first

    def span(b):
        return pl.ds(pl.multiple_of(b * blk, blk), blk)

    def part(i, c, b):
        return split(proj[i, span(b), mcols(c)])

    def push(own, into, send, recv, i, tp, ts):
        return remote(own.at[i], into.at[ts, i], send.at[i, tp], recv.at[i, ts], (at(tp, h), e))

    s_refs = (s_own, s_in, ssend, srecv)
    r_refs = (r_own, r_in, rsend, rrecv)
    zero = jnp.zeros((HD, HD), jnp.float32)

    def push_later(refs, i):
        @pl.when((t == 0) & (turns > 1))
        def _():
            push(*refs, i, 1, t).start()

    def earlier(refs, i):
        def add(ts, sum_):
            push(*refs, i, (t + 1) % turns, ts).wait_recv()
            return sum_ + refs[1][ts, i]

        sum_ = lax.fori_loop(jnp.maximum(t - 1, 0), t, add, zero)

        @pl.when((t > 0) & (t + 1 < turns))
        def _():
            refs[0][i] += sum_
            push(*refs, i, t + 1, t).start()

        return sum_

    def key_moments(i):
        def step(b, sum_):
            k = part(i, 1, b)
            return sum_ + dot(k, k, TN)
        s_own[i] = over_blocks(step, zero)
        push_later(s_refs, i)

    def local_keys(i):
        def step(b, sum_):
            q, k = part(i, 0, b), part(i, 1, b)
            scores = jnp.where(causal, dot(q, k, NT), 0.0)
            ubuf[i, span(b), :] = dot(split(scores), k, NN) + dot(q, split(sum_), NN)
            return sum_ + dot(k, k, TN)
        over_blocks(step, zero)

    def all_keys(i):
        before = split(earlier(s_refs, i))

        def step(b, sum_):
            u = ubuf[i, span(b), :] + dot(part(i, 0, b), before, NN)
            ubuf[i, span(b), :] = u
            return sum_ + dot(split(u), part(i, 2, b), TN)
        r_own[i] = over_blocks(step, zero)
        push_later(r_refs, i)

    def local_raw(i):
        def step(b, sum_):
            q, v, u = part(i, 0, b), part(i, 2, b), split(ubuf[i, span(b), :])
            scores = jnp.where(causal, dot(q, u, NT), 0.0)
            raw[i, span(b), :] = dot(split(scores), v, NN) + dot(q, split(sum_), NN)
            return sum_ + dot(u, v, TN)
        over_blocks(step, zero)

    def give(i, j, hh):
        hp = ring(j)
        return remote(
            result.at[i, tok(hp), :], landed.at[:, hcols(hh, i)], osend.at[i, j], orecv.at[i, hh],
            (at(t, hp), e),
        )

    def o_own(i):
        return pltpu.make_async_copy(
            result.at[i, tok(h), :], landed.at[:, hcols(h, i)], own_sem.at[heads, 1 + i]
        )

    def finish(i):
        before = split(earlier(r_refs, i))
        gain = gain_ref[:, hcols(h, i)]
        for j in list(range(1, group)) + [0]:
            rs = tok(ring(j))
            full = raw[i, rs, :] + dot(split(proj[i, rs, mcols(0)]), before, NN)
            mean_sq = jnp.mean(full * full, axis=-1, keepdims=True)
            result[i, rs, :] = (full * lax.rsqrt(mean_sq + epsilon) * gain).astype(jnp.bfloat16)
            (give(i, j, h) if j else o_own(i)).start()

    for i in range(heads):
        for c in order:
            w_own(i, c).start()
            for j in range(1, group):
                across(i, c, j, me).start()
    stages = (key_moments, local_keys, all_keys, local_raw, finish)
    if turns <= 8 and depth % 128 == 0:
        start_plane(0)
        start_tokens()
        for d in range(1, turns - 1):
            arrive(0, d)
        if heads > 1:
            start_plane(1)
        finish_tokens()
        for d in range(turns):
            if d == turns - 1 and d > 0:
                arrive(0, d)
            multiply_at(0, d)
        for i in range(heads):
            fill = []
            if i + 1 < heads:
                for d in range(turns):
                    if d + 1 < turns:
                        fill.append(functools.partial(arrive, i + 1, d + 1))
                    fill.append(functools.partial(multiply_at, i + 1, d))
            late = len(fill) - 4
            for stage in stages:
                stage(i)
                if len(fill) > late and len(fill) > 4:
                    fill.pop(0)()
                if stage is local_raw and i + 2 < heads:
                    start_plane(i + 2)
            for f in fill:
                f()
    else:
        start_tokens()
        for i in range(heads):
            start_plane(i)

            @pl.loop(1, turns)
            def _(d):
                arrive(i, d)
        finish_tokens()
        for i in range(heads):
            @pl.loop(0, group)
            def _(m):
                proj[i, tok(m), :] = lax.dot_general(
                    xbuf[tok(m), :], wbuf[i], NN, preferred_element_type=jnp.float32
                )
        for i in range(heads):
            for stage in stages:
                stage(i)

    for j in range(1, group):
        xacross(j, h).wait_send()
    for j in range(group):
        for o in range(1, peers):
            xsibling(j, o, e).wait_send()
    for i in range(heads):
        for c in order:
            for j in range(1, group):
                across(i, c, j, me).wait_send()

            @pl.when(t + 1 < turns)
            def _():
                @pl.loop(0, t + 1)
                def _(ts):
                    up(i, c, ts).wait_send()

            @pl.when(t > 0)
            def _():
                @pl.loop(t, turns)
                def _(ts):
                    down(i, c, ts).wait_send()

        @pl.when(t + 1 < turns)
        def _():
            push(*s_refs, i, t + 1, t).wait_send()
            push(*r_refs, i, t + 1, t).wait_send()

        o_own(i).wait()
        for j in range(1, group):
            give(i, j, h).wait_send()
            give(i, j, ring(j)).wait_recv()
    out_ref[...] = landed[...]


def body(tokens, qkv_weight, out_gain):
    n, peers = lax.axis_size("ctx"), lax.axis_size("head")
    toks, feats = tokens.shape
    rows, _, cols = qkv_weight.shape
    group = math.gcd(math.gcd(n, cols // HD), GROUP)
    turns = n // group
    width = cols // group
    heads = width // HD
    total = toks * group
    moments = (heads, HD, HD)
    f32, bf16 = jnp.float32, jnp.bfloat16
    dma = pltpu.SemaphoreType.DMA
    vmem = pl.BlockSpec(memory_space=pltpu.VMEM)
    return pl.pallas_call(
        functools.partial(kernel, n, peers, group),
        out_shape=jax.ShapeDtypeStruct((toks, cols), bf16),
        in_specs=[pl.BlockSpec(memory_space=pl.ANY)] * 2 + [vmem],
        out_specs=vmem,
        scratch_shapes=[
            pltpu.VMEM((total, feats * peers), bf16),
            pltpu.VMEM((heads, rows * n, 3 * HD), bf16),
            pltpu.VMEM((heads, total, 3 * HD), f32),
            pltpu.VMEM((heads, total, HD), f32),
            pltpu.VMEM((heads, total, HD), f32),
            pltpu.VMEM(moments, f32),
            pltpu.VMEM((turns,) + moments, f32),
            pltpu.VMEM(moments, f32),
            pltpu.VMEM((turns,) + moments, f32),
            pltpu.VMEM((heads, total, HD), bf16),
            pltpu.VMEM((toks, cols), bf16),
            dma((heads + 1, max(3, heads + 1))),
            dma((heads, 3, group)),
            dma((heads, 3, group)),
            dma((heads, 3, turns)),
            dma((heads, 3, turns)),
            dma((heads, 3, turns)),
            dma((group, peers)),
            dma((group,)),
            dma((group, peers)),
            dma((heads, turns)),
            dma((heads, turns)),
            dma((heads, turns)),
            dma((heads, turns)),
            dma((heads, group)),
            dma((heads, group)),
        ],
        compiler_params=pltpu.CompilerParams(
            collective_id=0, has_side_effects=True, vmem_limit_bytes=48 * 1024 * 1024
        ),
    )(tokens, qkv_weight.transpose(1, 0, 2), out_gain.reshape(1, cols))


def solution(mesh):
    in_specs = (P("ctx", "head"), P("ctx", None, "head"), P("head"))
    out_specs = P("ctx", "head")
    return jax.shard_map(body, mesh=mesh, in_specs=in_specs, out_specs=out_specs, check_vma=False)
```
